32 devices in a mesh: ep: 32 (over z, y, x, core), dp: 1.
Axes of the slice: x: 2, y: 2, z: 4, core: 2. Of those that a mesh axis runs over, the one named last changes fastest.
Arguments:
- tokens: bfloat16 [768, 3584], P(('ep', 'dp')), may hold values from -6 to 6
- grad_out: bfloat16 [768, 3584], P(('ep', 'dp')), may hold values from -0.29882812 to 0.29882812
- routes: int32 [768, 2], P(('ep', 'dp')), may hold values from 0 to 3, all different within a row; in each aligned block of 24 rows (0 to 23, 24 to 47, ...) at most 16 rows name the same one
- route_probs: float32 [768, 2], P(('ep', 'dp')), may hold values from 0.1 to 1
- gate_weight: bfloat16 [32, 3584, 128], P('ep', 'dp'), may hold values from -0.09375 to 0.09375
- up_weight: bfloat16 [32, 3584, 128], P('ep', 'dp'), may hold values from -0.09375 to 0.09375
- down_weight: bfloat16 [32, 3584, 128], P('ep', 'dp'), may hold values from -0.1875 to 0.1875
Outputs:
- grad_tokens: bfloat16 [768, 3584], P(('ep', 'dp'))
- grad_probs: float32 [768, 2], P(('ep', 'dp'))
- grad_gate: bfloat16 [32, 3584, 128], P('ep', 'dp')
- grad_up: bfloat16 [32, 3584, 128], P('ep', 'dp')
- grad_down: bfloat16 [32, 3584, 128], P('ep', 'dp')
The draws below stay inside these ranges and needn't reach their ends.
Inputs may be any that keep to these rules, and one draw needn't show every extreme that they name: `routes`: each row names 2 different experts. Within each aligned block of 24 rows (the tokens of one device) no expert is named by more than 16 rows; in some blocks one expert is named by exactly 16 rows.
All inputs are finite; a program needn't handle non-finite values.
Results may differ from the reference program's by a relative error of at most 0.017.
Values may be sent and summed in bfloat16 or wider, within the bound.
A program may use at most 64 MiB of HBM per device.

```python
import math
import jax
import jax.numpy as jnp
import numpy as np
from jax import lax

D = 3584
HIDDEN_SIZE = 1024
GROUP = 8
TOP = 2
TOK_DEV = 24
EXPERTS = 4
HID_DEV = 128
SLICES = 32
CAP = 16
TOKENS = 768
N_EP = 32
N_DP = 1


def shard_levels(stream_key, dims, shards, low, largest):
    loudness, own = 1.0, jax.random.fold_in(stream_key, 6)
    for position, parts in shards:
        draws = jnp.exp(jax.random.uniform(jax.random.fold_in(own, position), (parts,), jnp.float32, low / len(shards), largest / len(shards)))
        loudness = loudness * jnp.repeat(draws, dims[position] // parts).reshape([-1 if axis == position else 1 for axis in range(len(dims))])
    return loudness


def routed_block(rng, own, number, rows, number_of, top, reach, lean):
    sequence = jax.random.permutation(rng, number_of)
    heavy_load, usual = shares(number_of, rows * top, reach, lean, True), shares(number_of, rows * top, reach, lean, False)
    places = jnp.arange(number_of)

    def named(lengths, rotation):
        used = int((lengths > 0).sum())
        fixed = max(1, used // 4)
        moved = fixed + (places - fixed + rotation * (used - fixed)) % max(1, number_of - fixed)
        return jnp.zeros((number_of,), jnp.int32).at[sequence[jnp.where(places < fixed, places, moved)]].set(jnp.asarray(lengths, jnp.int32))

    lengths = jnp.where(number % 4 == 0, named(heavy_load, number // 4), named(usual, number - number // 4 - 1))
    mixed = jax.random.permutation(jax.random.fold_in(own, 3), number_of)
    source_of, receiver = mixed[0:number_of // 2 * 2:2], mixed[1:number_of // 2 * 2:2]
    room = jnp.minimum(lengths[source_of] - 1, reach - lengths[receiver]) // 2
    room = jnp.where((source_of == sequence[0]) | (receiver == sequence[0]) | (lengths[receiver] == 0), 0, jnp.maximum(room, 0))
    moved = jax.random.randint(jax.random.fold_in(own, 4), (number_of // 2,), 0, 1 << 20) % (room + 1)
    lengths = lengths.at[source_of].add(-moved).at[receiver].add(moved)
    members = jnp.searchsorted(jnp.cumsum(lengths), jnp.arange(rows * top), side="right").astype(jnp.int32)
    grid = members.reshape(top, rows).T
    grid = grid[jax.random.permutation(jax.random.fold_in(own, 1), rows)]
    rotation = jax.random.randint(jax.random.fold_in(own, 2), (rows, 1), 0, top)
    return jnp.take_along_axis(grid, (jnp.arange(top)[None, :] + rotation) % top, axis=1)


def shares(count, total, limit, slope, full):
    weights = [(1 << 20) // math.isqrt(grade ** slope) + 1 for grade in range(1, count + 1)]
    largest = limit if full else min(limit, max(-(-total // count), total * weights[0] // sum(weights)))
    least = 1 if total - largest >= count - 1 else 0
    holding, surplus = [largest] + [least] * (count - 1), total - largest - least * (count - 1)
    while surplus > 0:
        free = [i for i in range(1, count) if holding[i] < largest] or [i for i in range(1, count) if holding[i] < limit]
        mass, left = sum([weights[i] for i in free]), surplus
        for i in free:
            addition = min(limit - holding[i], max(1, left * weights[i] // mass), surplus)
            holding[i] = holding[i] + addition
            surplus = surplus - addition
    return np.array(holding)


def noise(key, shape, spread, limit, cuts=(), kind=jnp.bfloat16):
    entries = jax.random.normal(key, shape, jnp.float32) * spread
    if len(cuts) > 0:
        entries = shard_levels(key, shape, cuts, -0.22, 0.18) * entries
    return jnp.clip(entries, min=-limit, max=limit).astype(kind)


def setup_inputs(seed: int = 0) -> dict:
    streams_of = jax.random.split(jax.random.key(seed), 8)
    tokens = noise(streams_of[0], (TOKENS, D), 1.0, 6.0, ((0, 32),))
    grad_out = noise(streams_of[1], (TOKENS, D), 0.05, 0.29882812, ((0, 32),))
    routes_keys = jax.random.split(jax.random.fold_in(streams_of[2], 1), TOKENS // TOK_DEV)
    routes_turns = jax.random.permutation(jax.random.fold_in(streams_of[2], 3), TOKENS // TOK_DEV)
    routes = jax.vmap(lambda own, number: routed_block(jax.random.fold_in(streams_of[2], 2), own, number, TOK_DEV, EXPERTS, TOP, CAP, 2))(routes_keys, routes_turns).reshape((TOKENS, TOP))
    route_probs = jnp.clip(0.1 + 0.9 * jax.random.uniform(streams_of[3], (TOKENS, TOP), jnp.float32) ** shard_levels(streams_of[3], (TOKENS, TOP), ((0, 32),), -0.2, 0.2), 0.1, 1.0)
    gate_weight = noise(streams_of[4], (SLICES, D, HID_DEV), D ** -0.5, 0.09375, ((0, 32),))
    up_weight = noise(streams_of[5], (SLICES, D, HID_DEV), D ** -0.5, 0.09375, ((0, 32),))
    down_weight = noise(streams_of[6], (SLICES, D, HID_DEV), HIDDEN_SIZE ** -0.5, 0.1875, ((0, 32),))
    return {"tokens": tokens, "grad_out": grad_out, "routes": routes, "route_probs": route_probs, "gate_weight": gate_weight, "up_weight": up_weight, "down_weight": down_weight}


CONTRACT_HIDDEN = (((1,), (1,)), ((), ()))
CONTRACT_ROWS = (((0,), (0,)), ((), ()))


def slot_table(routes):
    copies = TOKENS * TOP
    blocks = N_EP * N_DP
    block_routes = routes.reshape(blocks, TOK_DEV * TOP)
    onehot = (block_routes[:, :, None] == jnp.arange(EXPERTS, dtype=jnp.int32)[None, None, :]).astype(jnp.int32)
    earlier = jnp.cumsum(onehot, axis=1) - onehot
    slot_rank = jnp.sum(earlier * onehot, axis=2)
    block_ids = jnp.arange(blocks, dtype=jnp.int32)[:, None] * jnp.ones((1, TOK_DEV * TOP), jnp.int32)
    row_place = (block_ids // N_DP) * CAP + slot_rank
    group_place = block_ids % N_DP
    table = jnp.full((EXPERTS, N_DP, N_EP * CAP), copies, jnp.int32)
    return table.at[block_routes.reshape(-1), group_place.reshape(-1), row_place.reshape(-1)].set(
        jnp.arange(copies, dtype=jnp.int32))


def expert_full(weight, expert):
    blocks_of = lax.dynamic_slice_in_dim(weight, (expert * GROUP).astype(jnp.int32), GROUP, 0)
    return jnp.transpose(blocks_of, (1, 0, 2)).reshape(D, HIDDEN_SIZE)


def reference(tokens, grad_out, routes, route_probs, gate_weight, up_weight, down_weight):
    copies = TOKENS * TOP
    table = slot_table(routes)
    flat_probs = route_probs.reshape(-1)

    def expert_step(carry, expert):
        gate_full = expert_full(gate_weight, expert)
        up_full = expert_full(up_weight, expert)
        down_full = expert_full(down_weight, expert)
        gate_split = gate_full.astype(jnp.float32).reshape(D, GROUP, HID_DEV)
        up_split = up_full.astype(jnp.float32).reshape(D, GROUP, HID_DEV)

        def group_step(inner, group_index):
            token_acc, score_acc, grad_acc = inner
            copy_ids = table[expert, group_index]
            valid = copy_ids < copies
            safe_ids = jnp.where(valid, copy_ids, 0)
            token_ids = safe_ids // TOP
            rows_in = jnp.where(valid[:, None], tokens[token_ids], jnp.zeros((), tokens.dtype))
            rows_grad = jnp.where(valid[:, None], grad_out[token_ids], jnp.zeros((), grad_out.dtype))
            rows_prob = jnp.where(valid, flat_probs[safe_ids], jnp.zeros((), flat_probs.dtype))
            gate_pre = jnp.dot(rows_in, gate_full, preferred_element_type=jnp.float32)
            up_pre = jnp.dot(rows_in, up_full, preferred_element_type=jnp.float32)
            sigmoid_gate = jax.nn.sigmoid(gate_pre)
            activated = gate_pre * sigmoid_gate
            hidden = (activated * up_pre).astype(jnp.bfloat16)
            scaled = (rows_prob[:, None] * rows_grad.astype(jnp.float32)).astype(jnp.bfloat16)
            down_grad = jnp.dot(rows_grad, down_full, preferred_element_type=jnp.float32)
            scores = jnp.sum(hidden.astype(jnp.float32) * down_grad, axis=1)
            hidden_grad = rows_prob[:, None] * down_grad
            gate_grad = (hidden_grad * up_pre * sigmoid_gate * (1.0 + gate_pre * (1.0 - sigmoid_gate))).astype(jnp.bfloat16)
            up_grad = (hidden_grad * activated).astype(jnp.bfloat16)
            slice_terms = jnp.einsum("rgh,dgh->rgd", gate_grad.astype(jnp.float32).reshape(-1, GROUP, HID_DEV), gate_split)
            slice_terms = slice_terms + jnp.einsum("rgh,dgh->rgd", up_grad.astype(jnp.float32).reshape(-1, GROUP, HID_DEV), up_split)
            rounded = lax.optimization_barrier(slice_terms.astype(jnp.bfloat16))
            token_rows = jnp.sum(rounded.astype(jnp.float32), axis=1)
            token_acc = token_acc.at[token_ids].add(jnp.where(valid[:, None], token_rows, 0.0))
            score_acc = score_acc.at[safe_ids].add(jnp.where(valid, scores, 0.0))
            gate_term = lax.dot_general(rows_in, gate_grad, CONTRACT_ROWS, preferred_element_type=jnp.float32)
            up_term = lax.dot_general(rows_in, up_grad, CONTRACT_ROWS, preferred_element_type=jnp.float32)
            down_term = lax.dot_general(scaled, hidden, CONTRACT_ROWS, preferred_element_type=jnp.float32)
            terms = lax.optimization_barrier(jnp.stack([gate_term, up_term, down_term]).astype(jnp.bfloat16))
            return (token_acc, score_acc, grad_acc + terms.astype(jnp.float32)), None

        token_acc, score_acc = carry
        start_grads = jnp.zeros((3, D, HIDDEN_SIZE), jnp.float32)
        (token_acc, score_acc, grad_acc), _ = lax.scan(
            group_step, (token_acc, score_acc, start_grads), jnp.arange(N_DP, dtype=jnp.int32))
        grads = grad_acc.astype(jnp.bfloat16).reshape(3, D, GROUP, HID_DEV).transpose(0, 2, 1, 3)
        return (token_acc, score_acc), grads

    start = (jnp.zeros((TOKENS, D), jnp.float32), jnp.zeros((copies,), jnp.float32))
    (token_acc, score_acc), stacked = lax.scan(expert_step, start, jnp.arange(EXPERTS, dtype=jnp.int32))
    grad_tokens = token_acc.astype(jnp.bfloat16)
    grad_probs = score_acc.reshape(TOKENS, TOP)
    grad_gate = stacked[:, 0].reshape(SLICES, D, HID_DEV)
    grad_up = stacked[:, 1].reshape(SLICES, D, HID_DEV)
    grad_down = stacked[:, 2].reshape(SLICES, D, HID_DEV)
    return (grad_tokens, grad_probs, grad_gate, grad_up, grad_down)
```

```python
import functools

import jax
import jax.numpy as jnp
from jax import lax
from jax.experimental import pallas as pl
from jax.experimental.pallas import tpu as pltpu
from jax.sharding import PartitionSpec as P

GROUP = 8
TOP = 2
LANES = 128
ROWS = 16
F32 = jnp.float32
BF16 = jnp.bfloat16
MESH = pl.DeviceIdType.MESH


def dot(a, b, ca, cb):
    return lax.dot_general(a, b, (((ca,), (cb,)), ((), ())), preferred_element_type=F32)


def fwd_label(k, kind):
    return k * 16 + kind


def kernel(
    experts,
    cap,
    tokens,
    grads,
    routes,
    probs,
    wg_hbm,
    wu_hbm,
    wd_hbm,
    out_tokens,
    out_probs,
    out_gate,
    out_up,
    out_down,
    xs,
    gs,
    x,
    g,
    sc,
    t,
    rcore,
    rxa,
    rxb,
    rya,
    ryb,
    rf1,
    rf2,
    o,
    wgu,
    wd,
    gut,
    hid,
    wsem,
    ssem,
    rsem,
):
    feats = tokens.shape[1]
    wide = feats + LANES
    r = experts * cap
    h1 = (wide // LANES + 1) // 2 * LANES
    hidden = wd.shape[1]
    me = lax.axis_index("ep")
    z = me // GROUP
    m = me % GROUP
    core = m % 2
    chip = m // 2
    xbit = chip % 2
    ybit = chip // 2
    chip_x = ybit * 2 + (1 - xbit)
    chip_y = (1 - ybit) * 2 + xbit
    chip_d = (1 - ybit) * 2 + (1 - xbit)
    base = z * GROUP
    dev_c = base + chip * 2 + (1 - core)
    dev_x = base + chip_x * 2 + core
    dev_y = base + chip_y * 2 + core

    def zof(k):
        val = z
        bit = 1
        while bit < experts:
            if k & bit:
                val = val + bit - 2 * bit * ((z // bit) % 2)
            bit *= 2
        return val

    zs = [zof(k) for k in range(experts)]
    dev_z = [zs[k] * GROUP + m for k in range(experts)]

    loads = [
        pltpu.make_async_copy(wg_hbm, wgu.at[:, pl.ds(0, hidden)], wsem.at[0]),
        pltpu.make_async_copy(wu_hbm, wgu.at[:, pl.ds(hidden, hidden)], wsem.at[1]),
        pltpu.make_async_copy(wd_hbm, wd, wsem.at[2]),
    ]
    for c in loads:
        c.start()

    barrier = pltpu.get_barrier_semaphore()
    friends = [dev_c, dev_x, dev_y] + dev_z[1:]
    for d in friends:
        pl.semaphore_signal(barrier, inc=1, device_id={"ep": d}, device_id_type=MESH)

    toks = tokens.shape[0]
    col = lax.broadcasted_iota(jnp.int32, (toks, r), 1)
    cole = col // cap
    cols = (col % cap).astype(F32)
    on0 = routes[:, 0:1] == cole
    on1 = routes[:, 1:2] == cole
    named = jnp.where(on0 | on1, 1.0, 0.0).astype(F32)
    lower = jnp.where(
        lax.broadcasted_iota(jnp.int32, (toks, toks), 1)
        < lax.broadcasted_iota(jnp.int32, (toks, toks), 0),
        1.0,
        0.0,
    ).astype(BF16)
    rank = dot(lower, named.astype(BF16), 1, 0)
    place = jnp.where(rank == cols, named, 0.0)
    place16 = place.astype(BF16)
    weight = place * (jnp.where(on0, probs[:, 0:1], 0.0) + jnp.where(on1, probs[:, 1:2], 0.0))
    high = weight.astype(BF16)
    low = (weight - high.astype(F32)).astype(BF16)
    ones = jnp.ones((toks, LANES), BF16)
    lane = lax.broadcasted_iota(jnp.int32, (r, LANES), 1)
    xs[:, :feats] = dot(place16, tokens[...], 0, 0).astype(BF16)
    xs[:, feats:] = jnp.where(lane < LANES // 2, dot(high, ones, 0, 0), dot(low, ones, 0, 0)).astype(BF16)
    gs[...] = dot(place16, grads[...], 0, 0).astype(BF16)

    started = []

    def send(label, src, dst, device):
        c = pltpu.make_async_remote_copy(
            src_ref=src,
            dst_ref=dst,
            send_sem=ssem.at[label],
            recv_sem=rsem.at[label],
            device_id={"ep": device},
            device_id_type=MESH,
        )
        c.start()
        started.append(c)
        return c

    def rows(zk, of_core):
        return pl.ds(pl.multiple_of(of_core * r + zk * cap, ROWS), cap)

    def slot(zk):
        return pl.ds(pl.multiple_of(zk * cap, ROWS), cap)

    pl.semaphore_wait(barrier, len(friends))

    first = {}
    for k in range(1, experts):
        there = rows(z, core)
        first[k] = (
            send(fwd_label(k, 0), xs.at[slot(zs[k])], x.at[chip, there], dev_z[k]),
            send(fwd_label(k, 1), gs.at[slot(zs[k])], g.at[chip, there], dev_z[k]),
        )
    x[chip, rows(z, core), :] = xs[slot(z), :]
    g[chip, rows(z, core), :] = gs[slot(z), :]

    own, diag, fromcore = {}, {}, {}
    for step in range(experts + 2):
        k = step
        if k < experts:
            if k > 0:
                first[k][0].wait_recv()
                first[k][1].wait_recv()
            at = rows(zs[k], core)
            xr, gr = x.at[chip, at], g.at[chip, at]
            own[k] = (
                send(fwd_label(k, 2), xr, xr, dev_x),
                send(fwd_label(k, 5), gr, gr, dev_y),
                send(fwd_label(k, 3), gr, gr, dev_x),
                send(fwd_label(k, 4), xr, xr, dev_y),
            )
            fromcore[0, k] = (
                send(fwd_label(k, 6), xr, xr, dev_c),
                send(fwd_label(k, 7), gr, gr, dev_c),
            )
        k = step - 1
        if 0 <= k < experts:
            at = rows(zs[k], core)
            xx, gx = x.at[chip_x, at], g.at[chip_x, at]
            xy, gy = x.at[chip_y, at], g.at[chip_y, at]
            own[k][0].wait_recv()
            dx = send(fwd_label(k, 8), xx, xx, dev_y)
            own[k][1].wait_recv()
            dg = send(fwd_label(k, 9), gy, gy, dev_x)
            own[k][2].wait_recv()
            own[k][3].wait_recv()
            diag[k] = (dx, dg)
            fromcore[1, k] = (
                send(fwd_label(k, 10), xx, xx, dev_c),
                send(fwd_label(k, 11), gx, gx, dev_c),
            )
            fromcore[2, k] = (
                send(fwd_label(k, 12), xy, xy, dev_c),
                send(fwd_label(k, 13), gy, gy, dev_c),
            )
        k = step - 2
        if 0 <= k < experts:
            at = rows(zs[k], core)
            xd, gd = x.at[chip_d, at], g.at[chip_d, at]
            diag[k][0].wait_recv()
            diag[k][1].wait_recv()
            fromcore[3, k] = (
                send(fwd_label(k, 14), xd, xd, dev_c),
                send(fwd_label(k, 15), gd, gd, dev_c),
            )

    for c in loads:
        c.wait()

    tile = 512 if feats % 512 == 0 else LANES
    n_tiles = feats // tile
    chips = (chip, chip_x, chip_y, chip_d)
    back = experts * 16
    cores = {}
    for q in (3, 1, 2, 0):
        for k in range(experts):
            for c in fromcore[q, k]:
                c.wait_recv()
        cq = chips[q]
        pre = dot(x[cq, :, :feats], wgu[...], 1, 0)
        down = dot(g[cq], wd[...], 1, 0)
        tail = x[cq, :, feats:].astype(F32)
        prob = tail[:, 0:1] + tail[:, LANES // 2 : LANES // 2 + 1]
        gate, up = pre[:, :hidden], pre[:, hidden:]
        sig = jax.nn.sigmoid(gate)
        act = gate * sig
        hid_q = (act * up).astype(BF16)
        score = jnp.sum(hid_q.astype(F32) * down, axis=1, keepdims=True)
        hg = prob * down
        ggrad = (hg * up * sig * (1.0 + gate * (1.0 - sig))).astype(BF16)
        ugrad = (hg * act).astype(BF16)
        both = jnp.concatenate([ggrad, ugrad], axis=1)
        t[cq, :, feats:] = jnp.broadcast_to(score, (2 * r, LANES)).astype(BF16)
        lanes = pl.ds(pl.multiple_of(cq * (2 * r), LANES), 2 * r)
        gut[:, lanes] = both.T
        hid[:, lanes] = hid_q.T

        def part(i, _):
            at = pl.ds(pl.multiple_of(i * tile, tile), tile)
            t[cq, :, at] = dot(both, wgu[at, :], 1, 1).astype(BF16)
            sc[cq, :, at] = (prob * g[cq, :, at].astype(F32)).astype(BF16)
            return 0

        lax.fori_loop(0, n_tiles, part, 0)
        away = pl.ds(pl.multiple_of((1 - core) * r, ROWS), r)
        cores[q] = send(back + q, t.at[cq, away], rcore.at[q], dev_c)

    left = pl.ds(0, h1)
    right = pl.ds(h1, wide - h1)
    back += 4
    hop1, hop2, home = {}, {}, {}
    for q in (3, 1, 2):
        cores[q].wait_recv()
    for k in range(experts - 1, -1, -1):
        at, zk = rows(zs[k], core), slot(zs[k])
        for q in (3, 1, 2):
            t[chips[q], at, :] = (
                t[chips[q], at, :].astype(F32) + rcore[q, zk, :].astype(F32)
            ).astype(BF16)
        b = back + 8 * k
        hop1[k] = (
            send(b, t.at[chip_d, at, left], rxb.at[zk], dev_x),
            send(b + 1, t.at[chip_d, at, right], ryb.at[zk], dev_y),
            send(b + 2, t.at[chip_x, at, left], rxa.at[zk], dev_x),
            send(b + 3, t.at[chip_y, at, right], rya.at[zk], dev_y),
        )

    def wgrad(i, _):
        at = pl.ds(pl.multiple_of(i * tile, tile), tile)
        res = dot(gut[...], x[:, :, at].reshape(8 * r, tile), 1, 0).astype(BF16).T
        out_gate[at, :] = res[:, :hidden]
        out_up[at, :] = res[:, hidden:]
        return 0

    lax.fori_loop(0, n_tiles, wgrad, 0)
    for k in range(experts - 1, -1, -1):
        at, zk = rows(zs[k], core), slot(zs[k])
        b = back + 8 * k
        hop1[k][0].wait_recv()
        t[chip_y, at, left] = (t[chip_y, at, left].astype(F32) + rxb[zk, :].astype(F32)).astype(BF16)
        s1 = send(b + 4, t.at[chip_y, at, left], rf1.at[zk], dev_y)
        hop1[k][1].wait_recv()
        t[chip_x, at, right] = (t[chip_x, at, right].astype(F32) + ryb[zk, :].astype(F32)).astype(BF16)
        s2 = send(b + 5, t.at[chip_x, at, right], rf2.at[zk], dev_x)
        hop2[k] = (s1, s2)

    def dgrad(i, _):
        at = pl.ds(pl.multiple_of(i * tile, tile), tile)
        out_down[at, :] = dot(hid[...], sc[:, :, at].reshape(8 * r, tile), 1, 0).astype(BF16).T
        return 0

    lax.fori_loop(0, n_tiles, dgrad, 0)
    cores[0].wait_recv()
    for k in range(experts - 1, -1, -1):
        at, zk = rows(zs[k], core), slot(zs[k])
        for c in (hop1[k][2], hop1[k][3], hop2[k][0], hop2[k][1]):
            c.wait_recv()
        mine = t[chip, at, :].astype(F32) + rcore[0, zk, :].astype(F32)
        lo = mine[:, :h1] + rxa[zk, :].astype(F32) + rf1[zk, :].astype(F32)
        hi = mine[:, h1:] + rya[zk, :].astype(F32) + rf2[zk, :].astype(F32)
        if k > 0:
            t[chip, at, left] = lo.astype(BF16)
            t[chip, at, right] = hi.astype(BF16)
            home[k] = send(back + 8 * k + 6, t.at[chip, at], o.at[slot(z)], dev_z[k])
        else:
            o[zk, left] = lo.astype(BF16)
            o[zk, right] = hi.astype(BF16)
    for k in range(1, experts):
        home[k].wait_recv()
    out_tokens[...] = dot(place16, o[:, :feats], 1, 0).astype(BF16)
    scores = o[:, feats:]
    s0 = dot(jnp.where(on0, place, 0.0).astype(BF16), scores, 1, 0)
    s1 = dot(jnp.where(on1, place, 0.0).astype(BF16), scores, 1, 0)
    lane = lax.broadcasted_iota(jnp.int32, (toks, LANES), 1)
    out_probs[...] = jnp.where(lane == 0, s0, s1)
    for c in started:
        c.wait_send()


def expert_call(experts, cap, tokens, grads, routes, probs, wg, wu, wd):
    toks, feats = tokens.shape
    hidden = wg.shape[1]
    r = experts * cap
    wide = feats + LANES
    h1 = (wide // LANES + 1) // 2 * LANES
    h2 = wide - h1
    vmem = pl.BlockSpec(memory_space=pltpu.VMEM)
    hbm = pl.BlockSpec(memory_space=pl.ANY)
    n_sem = experts * 16 + 4 + 8 * experts
    grad = jax.ShapeDtypeStruct((feats, hidden), BF16)
    return pl.pallas_call(
        functools.partial(kernel, experts, cap),
        out_shape=(
            jax.ShapeDtypeStruct((toks, feats), BF16),
            jax.ShapeDtypeStruct((toks, LANES), F32),
            grad,
            grad,
            grad,
        ),
        in_specs=[vmem] * 4 + [hbm] * 3,
        out_specs=(vmem,) * 5,
        scratch_shapes=[
            pltpu.VMEM((r, wide), BF16),
            pltpu.VMEM((r, feats), BF16),
            pltpu.VMEM((4, 2 * r, wide), BF16),
            pltpu.VMEM((4, 2 * r, feats), BF16),
            pltpu.VMEM((4, 2 * r, feats), BF16),
            pltpu.VMEM((4, 2 * r, wide), BF16),
            pltpu.VMEM((4, r, wide), BF16),
            pltpu.VMEM((r, h1), BF16),
            pltpu.VMEM((r, h1), BF16),
            pltpu.VMEM((r, h2), BF16),
            pltpu.VMEM((r, h2), BF16),
            pltpu.VMEM((r, h1), BF16),
            pltpu.VMEM((r, h2), BF16),
            pltpu.VMEM((r, wide), BF16),
            pltpu.VMEM((feats, 2 * hidden), BF16),
            pltpu.VMEM((feats, hidden), BF16),
            pltpu.VMEM((2 * hidden, 8 * r), BF16),
            pltpu.VMEM((hidden, 8 * r), BF16),
            pltpu.SemaphoreType.DMA((3,)),
            pltpu.SemaphoreType.DMA((n_sem,)),
            pltpu.SemaphoreType.DMA((n_sem,)),
        ],
        compiler_params=pltpu.CompilerParams(
            collective_id=0, has_side_effects=True, vmem_limit_bytes=58 * 2**20
        ),
    )(tokens, grads, routes, probs, wg, wu, wd)


def per_device(tokens, grad_out, routes, route_probs, gate_weight, up_weight, down_weight):
    tok_count = tokens.shape[0]
    experts = lax.axis_size("ep") // GROUP
    slots = min(
        tok_count // GROUP,
        max(1, (4 * TOP * tok_count + 3 * experts * GROUP - 1) // (3 * experts * GROUP)),
    )
    cap = -(-GROUP * slots // ROWS) * ROWS
    split = lax.axis_size("dp") > 1

    def whole(w):
        return lax.all_gather(w, "dp", axis=1, tiled=True)[0] if split else w[0]

    def shared(term):
        if split:
            term = lax.psum_scatter(term, "dp", scatter_dimension=0, tiled=True)
        return term.astype(BF16)[None]

    grad_tokens, probs, gate, up, down = expert_call(
        experts,
        cap,
        tokens,
        grad_out,
        routes,
        route_probs,
        whole(gate_weight),
        whole(up_weight),
        whole(down_weight),
    )
    return (grad_tokens, probs[:, :TOP], shared(gate), shared(up), shared(down))


def solution(mesh):
    rows = P(("ep", "dp"), None)
    blocks = P("ep", "dp", None)
    return jax.shard_map(
        per_device,
        mesh=mesh,
        in_specs=(rows,) * 4 + (blocks,) * 3,
        out_specs=(rows,) * 2 + (blocks,) * 3,
        check_vma=False,
    )
```

```python
import functools

import jax
import jax.numpy as jnp
from jax import lax
from jax.experimental import pallas as pl
from jax.experimental.pallas import tpu as pltpu
from jax.sharding import PartitionSpec as P

GROUP = 8
TOP = 2
LANES = 128
ROWS = 16
F32 = jnp.float32
BF16 = jnp.bfloat16
MESH = pl.DeviceIdType.MESH


def dot(a, b, ca, cb):
    return lax.dot_general(a, b, (((ca,), (cb,)), ((), ())), preferred_element_type=F32)


def fwd_label(k, kind):
    return k * 16 + kind


def kernel(
    experts,
    cap,
    tokens_hbm,
    grads_hbm,
    routes_hbm,
    probs_hbm,
    wg_hbm,
    wu_hbm,
    wd_hbm,
    out_tokens,
    out_probs,
    out_gate,
    out_up,
    out_down,
    xs,
    gs,
    x,
    g,
    sc,
    t,
    rcore,
    rxa,
    rxb,
    rya,
    ryb,
    rf1,
    rf2,
    o,
    wgu,
    wd,
    gut,
    hid,
    tokens,
    grads,
    routes,
    probs,
    wsem,
    ssem,
    rsem,
):
    feats = tokens.shape[1]
    wide = feats + LANES
    r = experts * cap
    h1 = (wide // LANES + 1) // 2 * LANES
    hidden = wd.shape[1]
    me = lax.axis_index("ep")
    z = me // GROUP
    m = me % GROUP
    core = m % 2
    chip = m // 2
    xbit = chip % 2
    ybit = chip // 2
    chip_x = ybit * 2 + (1 - xbit)
    chip_y = (1 - ybit) * 2 + xbit
    chip_d = (1 - ybit) * 2 + (1 - xbit)
    base = z * GROUP
    dev_c = base + chip * 2 + (1 - core)
    dev_x = base + chip_x * 2 + core
    dev_y = base + chip_y * 2 + core

    def zof(k):
        val = z
        bit = 1
        while bit < experts:
            if k & bit:
                val = val + bit - 2 * bit * ((z // bit) % 2)
            bit *= 2
        return val

    zs = [zof(k) for k in range(experts)]
    dev_z = [zs[k] * GROUP + m for k in range(experts)]

    inputs = [
        pltpu.make_async_copy(routes_hbm, routes, wsem.at[3]),
        pltpu.make_async_copy(probs_hbm, probs, wsem.at[4]),
        pltpu.make_async_copy(tokens_hbm, tokens, wsem.at[5]),
        pltpu.make_async_copy(grads_hbm, grads, wsem.at[6]),
    ]
    for c in inputs:
        c.start()
    loads = [
        pltpu.make_async_copy(wg_hbm, wgu.at[:, pl.ds(0, hidden)], wsem.at[0]),
        pltpu.make_async_copy(wu_hbm, wgu.at[:, pl.ds(hidden, hidden)], wsem.at[1]),
        pltpu.make_async_copy(wd_hbm, wd, wsem.at[2]),
    ]
    for c in loads:
        c.start()

    barrier = pltpu.get_barrier_semaphore()
    friends = [dev_c, dev_x, dev_y] + dev_z[1:]
    for d in friends:
        pl.semaphore_signal(barrier, inc=1, device_id={"ep": d}, device_id_type=MESH)

    for c in inputs:
        c.wait()
    toks = tokens.shape[0]
    slot_at = lax.broadcasted_iota(jnp.int32, (r, toks), 0)
    expert_at = slot_at // cap
    on0 = routes[0:1, :] == expert_at
    on1 = routes[1:2, :] == expert_at
    named = jnp.where(on0 | on1, 1.0, 0.0).astype(F32)
    upper = jnp.where(
        lax.broadcasted_iota(jnp.int32, (toks, toks), 0)
        < lax.broadcasted_iota(jnp.int32, (toks, toks), 1),
        1.0,
        0.0,
    ).astype(BF16)
    rank = dot(named.astype(BF16), upper, 1, 0)
    place = jnp.where(rank == (slot_at % cap).astype(F32), named, 0.0)
    place16 = place.astype(BF16)
    weight = place * jnp.where(on0, probs[0:1, :], probs[1:2, :])
    prob_of = jnp.sum(weight, axis=1, keepdims=True)
    high = prob_of.astype(BF16)
    low = (prob_of - high.astype(F32)).astype(BF16)
    lane = lax.broadcasted_iota(jnp.int32, (r, LANES), 1)
    xs[:, :feats] = dot(place16, tokens[...], 1, 0).astype(BF16)
    xs[:, feats:] = jnp.where(lane < LANES // 2, high.astype(F32), low.astype(F32)).astype(BF16)
    gs[...] = dot(place16, grads[...], 1, 0).astype(BF16)

    started = []

    def send(label, src, dst, device):
        c = pltpu.make_async_remote_copy(
            src_ref=src,
            dst_ref=dst,
            send_sem=ssem.at[label],
            recv_sem=rsem.at[label],
            device_id={"ep": device},
            device_id_type=MESH,
        )
        c.start()
        started.append(c)
        return c

    def rows(zk, of_core):
        return pl.ds(pl.multiple_of(of_core * r + zk * cap, ROWS), cap)

    def slot(zk):
        return pl.ds(pl.multiple_of(zk * cap, ROWS), cap)

    pl.semaphore_wait(barrier, len(friends))

    first = {}

    def exchange(k):
        there = rows(z, core)
        first[k] = (
            send(fwd_label(k, 0), xs.at[slot(zs[k])], x.at[chip, there], dev_z[k]),
            send(fwd_label(k, 1), gs.at[slot(zs[k])], g.at[chip, there], dev_z[k]),
        )

    for k in range(1, min(3, experts)):
        exchange(k)
    x[chip, rows(z, core), :] = xs[slot(z), :]
    g[chip, rows(z, core), :] = gs[slot(z), :]

    own, diag, fromcore = {}, {}, {}

    def spread(k):
        if k > 0:
            first[k][0].wait_recv()
            first[k][1].wait_recv()
            if k + 2 < experts:
                exchange(k + 2)
        at = rows(zs[k], core)
        xr, gr = x.at[chip, at], g.at[chip, at]
        own[k] = (
            send(fwd_label(k, 2), xr, xr, dev_x),
            send(fwd_label(k, 5), gr, gr, dev_y),
            send(fwd_label(k, 3), gr, gr, dev_x),
            send(fwd_label(k, 4), xr, xr, dev_y),
        )
        fromcore[0, k] = (
            send(fwd_label(k, 6), xr, xr, dev_c),
            send(fwd_label(k, 7), gr, gr, dev_c),
        )

    def relay(k):
        at = rows(zs[k], core)
        xx, gx = x.at[chip_x, at], g.at[chip_x, at]
        xy, gy = x.at[chip_y, at], g.at[chip_y, at]
        own[k][0].wait_recv()
        dx = send(fwd_label(k, 8), xx, xx, dev_y)
        own[k][1].wait_recv()
        dg = send(fwd_label(k, 9), gy, gy, dev_x)
        own[k][2].wait_recv()
        own[k][3].wait_recv()
        diag[k] = (dx, dg)
        fromcore[1, k] = (
            send(fwd_label(k, 10), xx, xx, dev_c),
            send(fwd_label(k, 11), gx, gx, dev_c),
        )
        fromcore[2, k] = (
            send(fwd_label(k, 12), xy, xy, dev_c),
            send(fwd_label(k, 13), gy, gy, dev_c),
        )

    def relay_diag(k):
        at = rows(zs[k], core)
        xd, gd = x.at[chip_d, at], g.at[chip_d, at]
        diag[k][0].wait_recv()
        diag[k][1].wait_recv()
        fromcore[3, k] = (
            send(fwd_label(k, 14), xd, xd, dev_c),
            send(fwd_label(k, 15), gd, gd, dev_c),
        )

    tile = 512 if feats % 512 == 0 else LANES
    n_tiles = feats // tile
    chips = (chip, chip_x, chip_y, chip_d)
    back = experts * 16
    cores = {}

    def compute(q):
        for k in range(experts):
            for c in fromcore[q, k]:
                c.wait_recv()
        cq = chips[q]
        pre = dot(x[cq, :, :feats], wgu[...], 1, 0)
        down = dot(g[cq], wd[...], 1, 0)
        tail = x[cq, :, feats:].astype(F32)
        prob = tail[:, 0:1] + tail[:, LANES // 2 : LANES // 2 + 1]
        gate, up = pre[:, :hidden], pre[:, hidden:]
        sig = jax.nn.sigmoid(gate)
        act = gate * sig
        hid_q = (act * up).astype(BF16)
        score = jnp.sum(hid_q.astype(F32) * down, axis=1, keepdims=True)
        hg = prob * down
        ggrad = (hg * up * sig * (1.0 + gate * (1.0 - sig))).astype(BF16)
        ugrad = (hg * act).astype(BF16)
        both = jnp.concatenate([ggrad, ugrad], axis=1)
        t[cq, :, feats:] = jnp.broadcast_to(score, (2 * r, LANES)).astype(BF16)
        lanes = pl.ds(pl.multiple_of(cq * (2 * r), LANES), 2 * r)
        gut[:, lanes] = both.T
        hid[:, lanes] = hid_q.T

        def part(i, _):
            at = pl.ds(pl.multiple_of(i * tile, tile), tile)
            t[cq, :, at] = dot(both, wgu[at, :], 1, 1).astype(BF16)
            sc[cq, :, at] = (prob * g[cq, :, at].astype(F32)).astype(BF16)
            return 0

        lax.fori_loop(0, n_tiles, part, 0)
        away = pl.ds(pl.multiple_of((1 - core) * r, ROWS), r)
        cores[q] = send(back + q, t.at[cq, away], rcore.at[q], dev_c)

    left = pl.ds(0, h1)
    right = pl.ds(h1, wide - h1)
    hops = back + 4
    hop1, hop2, home = {}, {}, {}
    mine_rows = pl.ds(pl.multiple_of(core * r, ROWS), r)

    def add_core(q):
        cores[q].wait_recv()
        t[chips[q], mine_rows, :] = (
            t[chips[q], mine_rows, :].astype(F32) + rcore[q].astype(F32)
        ).astype(BF16)

    for step in range(experts):
        spread(step)
        if step >= 1:
            relay(step - 1)
        if step >= 2:
            relay_diag(step - 2)
    for c in loads:
        c.wait()
    compute(0)
    relay(experts - 1)
    relay_diag(experts - 2)
    compute(1)
    relay_diag(experts - 1)
    compute(2)
    add_core(1)
    near_x = send(hops + 2, t.at[chip_x, mine_rows, left], rxa, dev_x)
    add_core(2)
    near_y = send(hops + 3, t.at[chip_y, mine_rows, right], rya, dev_y)
    compute(3)
    cores[3].wait_recv()
    for k in range(experts - 1, -1, -1):
        at, zk = rows(zs[k], core), slot(zs[k])
        t[chip_d, at, :] = (
            t[chip_d, at, :].astype(F32) + rcore[3, zk, :].astype(F32)
        ).astype(BF16)
        b = hops + 8 * k
        hop1[k] = (
            send(b, t.at[chip_d, at, left], rxb.at[zk], dev_x),
            send(b + 1, t.at[chip_d, at, right], ryb.at[zk], dev_y),
        )

    def wgrad(i, _):
        at = pl.ds(pl.multiple_of(i * tile, tile), tile)
        res = dot(gut[...], x[:, :, at].reshape(8 * r, tile), 1, 0).astype(BF16).T
        out_gate[at, :] = res[:, :hidden]
        out_up[at, :] = res[:, hidden:]
        return 0

    lax.fori_loop(0, n_tiles, wgrad, 0)
    for k in range(experts - 1, -1, -1):
        at, zk = rows(zs[k], core), slot(zs[k])
        b = hops + 8 * k
        hop1[k][0].wait_recv()
        t[chip_y, at, left] = (t[chip_y, at, left].astype(F32) + rxb[zk, :].astype(F32)).astype(BF16)
        s1 = send(b + 4, t.at[chip_y, at, left], rf1.at[zk], dev_y)
        hop1[k][1].wait_recv()
        t[chip_x, at, right] = (t[chip_x, at, right].astype(F32) + ryb[zk, :].astype(F32)).astype(BF16)
        s2 = send(b + 5, t.at[chip_x, at, right], rf2.at[zk], dev_x)
        hop2[k] = (s1, s2)

    def dgrad(i, _):
        at = pl.ds(pl.multiple_of(i * tile, tile), tile)
        out_down[at, :] = dot(hid[...], sc[:, :, at].reshape(8 * r, tile), 1, 0).astype(BF16).T
        return 0

    lax.fori_loop(0, n_tiles, dgrad, 0)
    cores[0].wait_recv()
    near_x.wait_recv()
    near_y.wait_recv()
    for k in range(experts - 1, -1, -1):
        at, zk = rows(zs[k], core), slot(zs[k])
        for c in hop2[k]:
            c.wait_recv()
        mine = t[chip, at, :].astype(F32) + rcore[0, zk, :].astype(F32)
        lo = mine[:, :h1] + rxa[zk, :].astype(F32) + rf1[zk, :].astype(F32)
        hi = mine[:, h1:] + rya[zk, :].astype(F32) + rf2[zk, :].astype(F32)
        if k > 0:
            t[chip, at, left] = lo.astype(BF16)
            t[chip, at, right] = hi.astype(BF16)
            home[k] = send(hops + 8 * k + 6, t.at[chip, at], o.at[slot(z)], dev_z[k])
        else:
            o[zk, left] = lo.astype(BF16)
            o[zk, right] = hi.astype(BF16)
    for k in range(1, experts):
        home[k].wait_recv()
    out_tokens[...] = dot(place16, o[:, :feats], 0, 0).astype(BF16)
    score = o[:, feats : feats + 1].astype(F32)
    out_probs[0:1, :] = jnp.sum(jnp.where(on0, place, 0.0) * score, axis=0, keepdims=True)
    out_probs[1:2, :] = jnp.sum(jnp.where(on1, place, 0.0) * score, axis=0, keepdims=True)
    for c in started:
        c.wait_send()


def write_out(*refs):
    count = len(refs) // 2
    sems = refs[-1]
    copies = [
        pltpu.make_async_copy(refs[i], refs[count + i], sems.at[i]) for i in range(count)
    ]
    for c in copies:
        c.start()
    for c in copies:
        c.wait()


def finish(arrays):
    arrays = [pltpu.with_memory_space_constraint(a, pltpu.VMEM) for a in arrays]
    return pl.pallas_call(
        write_out,
        out_shape=[jax.ShapeDtypeStruct(a.shape, a.dtype) for a in arrays],
        in_specs=[pl.BlockSpec(memory_space=pltpu.VMEM)] * len(arrays),
        out_specs=[pl.BlockSpec(memory_space=pl.ANY)] * len(arrays),
        scratch_shapes=[pltpu.SemaphoreType.DMA((len(arrays),))],
        compiler_params=pltpu.CompilerParams(has_side_effects=True, vmem_limit_bytes=2**20),
    )(*arrays)


def expert_call(place, limit, experts, cap, tokens, grads, routes, probs, wg, wu, wd):
    toks, feats = tokens.shape
    hidden = wg.shape[1]
    r = experts * cap
    wide = feats + LANES
    h1 = (wide // LANES + 1) // 2 * LANES
    h2 = wide - h1
    vmem = pl.BlockSpec(memory_space=pltpu.VMEM)
    hbm = pl.BlockSpec(memory_space=pltpu.HBM)
    n_sem = experts * 16 + 4 + 8 * experts
    grad = place((feats, hidden), BF16)
    return pl.pallas_call(
        functools.partial(kernel, experts, cap),
        out_shape=(
            place((toks, feats), BF16),
            place((TOP, toks), F32),
            grad,
            grad,
            grad,
        ),
        in_specs=[hbm] * 7,
        out_specs=(vmem,) * 5,
        scratch_shapes=[
            pltpu.VMEM((r, wide), BF16),
            pltpu.VMEM((r, feats), BF16),
            pltpu.VMEM((4, 2 * r, wide), BF16),
            pltpu.VMEM((4, 2 * r, feats), BF16),
            pltpu.VMEM((4, 2 * r, feats), BF16),
            pltpu.VMEM((4, 2 * r, wide), BF16),
            pltpu.VMEM((4, r, wide), BF16),
            pltpu.VMEM((r, h1), BF16),
            pltpu.VMEM((r, h1), BF16),
            pltpu.VMEM((r, h2), BF16),
            pltpu.VMEM((r, h2), BF16),
            pltpu.VMEM((r, h1), BF16),
            pltpu.VMEM((r, h2), BF16),
            pltpu.VMEM((r, wide), BF16),
            pltpu.VMEM((feats, 2 * hidden), BF16),
            pltpu.VMEM((feats, hidden), BF16),
            pltpu.VMEM((2 * hidden, 8 * r), BF16),
            pltpu.VMEM((hidden, 8 * r), BF16),
            pltpu.VMEM((toks, feats), BF16),
            pltpu.VMEM((toks, feats), BF16),
            pltpu.VMEM((TOP, toks), jnp.int32),
            pltpu.VMEM((TOP, toks), F32),
            pltpu.SemaphoreType.DMA((7,)),
            pltpu.SemaphoreType.DMA((n_sem,)),
            pltpu.SemaphoreType.DMA((n_sem,)),
        ],
        compiler_params=pltpu.CompilerParams(
            collective_id=0, has_side_effects=True, vmem_limit_bytes=limit
        ),
    )(tokens, grads, routes, probs, wg, wu, wd)


def per_device(tokens, grad_out, routes, route_probs, gate_weight, up_weight, down_weight):
    tok_count = tokens.shape[0]
    experts = lax.axis_size("ep") // GROUP
    slots = min(
        tok_count // GROUP,
        max(1, (4 * TOP * tok_count + 3 * experts * GROUP - 1) // (3 * experts * GROUP)),
    )
    cap = -(-GROUP * slots // ROWS) * ROWS
    split = lax.axis_size("dp") > 1

    def whole(w):
        return lax.all_gather(w, "dp", axis=1, tiled=True)[0] if split else w[0]

    def shared(term):
        if split:
            term = lax.psum_scatter(term, "dp", scatter_dimension=0, tiled=True)
        return term.astype(BF16)[None]

    made = expert_call(
        jax.ShapeDtypeStruct if split else pltpu.VMEM,
        58 * 2**20 if split else 64100000,
        experts,
        cap,
        tokens,
        grad_out,
        routes.T,
        route_probs.T,
        whole(gate_weight),
        whole(up_weight),
        whole(down_weight),
    )
    grad_tokens, probs, gate, up, down = made if split else finish(made)
    return (grad_tokens, probs.T, shared(gate), shared(up), shared(down))


def solution(mesh):
    rows = P(("ep", "dp"), None)
    blocks = P("ep", "dp", None)
    return jax.shard_map(
        per_device,
        mesh=mesh,
        in_specs=(rows,) * 4 + (blocks,) * 3,
        out_specs=(rows,) * 2 + (blocks,) * 3,
        check_vma=False,
    )
```

```python
import functools

import jax
import jax.numpy as jnp
from jax import lax
from jax.experimental import pallas as pl
from jax.experimental.pallas import tpu as pltpu
from jax.sharding import PartitionSpec as P

GROUP = 8
TOP = 2
LANES = 128
ROWS = 16
F32 = jnp.float32
BF16 = jnp.bfloat16
MESH = pl.DeviceIdType.MESH


def dot(a, b, ca, cb):
    return lax.dot_general(a, b, (((ca,), (cb,)), ((), ())), preferred_element_type=F32)


def fwd_label(k, kind):
    return k * 16 + kind


def kernel(
    experts,
    cap,
    tokens_hbm,
    grads_hbm,
    routes_hbm,
    probs_hbm,
    wg_hbm,
    wu_hbm,
    wd_hbm,
    out_tokens,
    out_probs,
    out_gate,
    out_up,
    out_down,
    xs,
    gs,
    x,
    g,
    t,
    rcore,
    rxa,
    rxb,
    rya,
    ryb,
    rf1,
    rf2,
    o,
    wgu,
    wd,
    gut,
    hid,
    tokens,
    grads,
    routes,
    probs,
    wsem,
    ssem,
    rsem,
):
    feats = tokens.shape[1]
    wide = feats + LANES
    r = experts * cap
    h1 = (wide // LANES + 1) // 2 * LANES
    hidden = wd.shape[1]
    me = lax.axis_index("ep")
    z = me // GROUP
    m = me % GROUP
    core = m % 2
    chip = m // 2
    xbit = chip % 2
    ybit = chip // 2
    chip_x = ybit * 2 + (1 - xbit)
    chip_y = (1 - ybit) * 2 + xbit
    chip_d = (1 - ybit) * 2 + (1 - xbit)
    base = z * GROUP
    dev_c = base + chip * 2 + (1 - core)
    dev_x = base + chip_x * 2 + core
    dev_y = base + chip_y * 2 + core

    def zof(k):
        val = z
        bit = 1
        while bit < experts:
            if k & bit:
                val = val + bit - 2 * bit * ((z // bit) % 2)
            bit *= 2
        return val

    zs = [zof(k) for k in range(experts)]
    dev_z = [zs[k] * GROUP + m for k in range(experts)]

    inputs = [
        pltpu.make_async_copy(routes_hbm, routes, wsem.at[3]),
        pltpu.make_async_copy(probs_hbm, probs, wsem.at[4]),
        pltpu.make_async_copy(tokens_hbm, tokens, wsem.at[5]),
        pltpu.make_async_copy(grads_hbm, grads, wsem.at[6]),
    ]
    for c in inputs:
        c.start()
    loads = [
        pltpu.make_async_copy(wg_hbm, wgu.at[:, pl.ds(0, hidden)], wsem.at[0]),
        pltpu.make_async_copy(wu_hbm, wgu.at[:, pl.ds(hidden, hidden)], wsem.at[1]),
        pltpu.make_async_copy(wd_hbm, wd, wsem.at[2]),
    ]
    for c in loads:
        c.start()

    barrier = pltpu.get_barrier_semaphore()
    friends = [dev_c, dev_x, dev_y] + dev_z[1:]
    for d in friends:
        pl.semaphore_signal(barrier, inc=1, device_id={"ep": d}, device_id_type=MESH)

    for c in inputs:
        c.wait()
    toks = tokens.shape[0]
    slot_at = lax.broadcasted_iota(jnp.int32, (r, toks), 0)
    expert_at = slot_at // cap
    on0 = routes[0:1, :] == expert_at
    on1 = routes[1:2, :] == expert_at
    named = jnp.where(on0 | on1, 1.0, 0.0).astype(F32)
    upper = jnp.where(
        lax.broadcasted_iota(jnp.int32, (toks, toks), 0)
        < lax.broadcasted_iota(jnp.int32, (toks, toks), 1),
        1.0,
        0.0,
    ).astype(BF16)
    rank = dot(named.astype(BF16), upper, 1, 0)
    place = jnp.where(rank == (slot_at % cap).astype(F32), named, 0.0)
    place16 = place.astype(BF16)
    weight = place * jnp.where(on0, probs[0:1, :], probs[1:2, :])
    prob_of = jnp.sum(weight, axis=1, keepdims=True)
    high = prob_of.astype(BF16)
    low = (prob_of - high.astype(F32)).astype(BF16)
    lane = lax.broadcasted_iota(jnp.int32, (r, LANES), 1)
    xs[:, :feats] = dot(place16, tokens[...], 1, 0).astype(BF16)
    xs[:, feats:] = jnp.where(lane < LANES // 2, high.astype(F32), low.astype(F32)).astype(BF16)
    gs[...] = dot(place16, grads[...], 1, 0).astype(BF16)

    started = []

    def send(label, src, dst, device):
        c = pltpu.make_async_remote_copy(
            src_ref=src,
            dst_ref=dst,
            send_sem=ssem.at[label],
            recv_sem=rsem.at[label],
            device_id={"ep": device},
            device_id_type=MESH,
        )
        c.start()
        started.append(c)
        return c

    def rows(zk, of_core):
        return pl.ds(pl.multiple_of(of_core * r + zk * cap, ROWS), cap)

    def slot(zk):
        return pl.ds(pl.multiple_of(zk * cap, ROWS), cap)

    pl.semaphore_wait(barrier, len(friends))

    first = {}

    def exchange(k):
        there = rows(z, core)
        first[k] = (
            send(fwd_label(k, 0), xs.at[slot(zs[k])], x.at[chip, there], dev_z[k]),
            send(fwd_label(k, 1), gs.at[slot(zs[k])], g.at[chip, there], dev_z[k]),
        )

    for k in range(1, min(3, experts)):
        exchange(k)
    x[chip, rows(z, core), :] = xs[slot(z), :]
    g[chip, rows(z, core), :] = gs[slot(z), :]

    own, diag, fromcore = {}, {}, {}

    def spread(k):
        if k > 0:
            first[k][0].wait_recv()
            first[k][1].wait_recv()
            if k + 2 < experts:
                exchange(k + 2)
        at = rows(zs[k], core)
        xr, gr = x.at[chip, at], g.at[chip, at]
        own[k] = (
            send(fwd_label(k, 2), xr, xr, dev_x),
            send(fwd_label(k, 5), gr, gr, dev_y),
            send(fwd_label(k, 3), gr, gr, dev_x),
            send(fwd_label(k, 4), xr, xr, dev_y),
        )
        fromcore[0, k] = (
            send(fwd_label(k, 6), xr, xr, dev_c),
            send(fwd_label(k, 7), gr, gr, dev_c),
        )

    def relay(k):
        at = rows(zs[k], core)
        xx, gx = x.at[chip_x, at], g.at[chip_x, at]
        xy, gy = x.at[chip_y, at], g.at[chip_y, at]
        own[k][0].wait_recv()
        dx = send(fwd_label(k, 8), xx, xx, dev_y)
        own[k][1].wait_recv()
        dg = send(fwd_label(k, 9), gy, gy, dev_x)
        own[k][2].wait_recv()
        own[k][3].wait_recv()
        diag[k] = (dx, dg)
        fromcore[1, k] = (
            send(fwd_label(k, 10), xx, xx, dev_c),
            send(fwd_label(k, 11), gx, gx, dev_c),
        )
        fromcore[2, k] = (
            send(fwd_label(k, 12), xy, xy, dev_c),
            send(fwd_label(k, 13), gy, gy, dev_c),
        )

    def relay_diag(k):
        at = rows(zs[k], core)
        xd, gd = x.at[chip_d, at], g.at[chip_d, at]
        diag[k][0].wait_recv()
        diag[k][1].wait_recv()
        fromcore[3, k] = (
            send(fwd_label(k, 14), xd, xd, dev_c),
            send(fwd_label(k, 15), gd, gd, dev_c),
        )

    tile = 512 if feats % 512 == 0 else LANES
    n_tiles = feats // tile
    chips = (chip, chip_x, chip_y, chip_d)
    back = experts * 16
    cores = {}

    def compute(q):
        for k in range(experts):
            for c in fromcore[q, k]:
                c.wait_recv()
        cq = chips[q]
        pre = dot(x[cq, :, :feats], wgu[...], 1, 0)
        down = dot(g[cq], wd[...], 1, 0)
        tail = x[cq, :, feats:].astype(F32)
        prob = tail[:, 0:1] + tail[:, LANES // 2 : LANES // 2 + 1]
        gate, up = pre[:, :hidden], pre[:, hidden:]
        sig = jax.nn.sigmoid(gate)
        act = gate * sig
        hid_q = (act * up).astype(BF16)
        score = jnp.sum(hid_q.astype(F32) * down, axis=1, keepdims=True)
        hg = prob * down
        ggrad = (hg * up * sig * (1.0 + gate * (1.0 - sig))).astype(BF16)
        ugrad = (hg * act).astype(BF16)
        both = jnp.concatenate([ggrad, ugrad], axis=1)
        t[cq, :, feats:] = jnp.broadcast_to(score, (2 * r, LANES)).astype(BF16)
        lanes = pl.ds(pl.multiple_of(cq * (2 * r), LANES), 2 * r)
        gut[:, lanes] = both.T
        hid[:, lanes] = hid_q.T

        def part(i, _):
            at = pl.ds(pl.multiple_of(i * tile, tile), tile)
            t[cq, :, at] = dot(both, wgu[at, :], 1, 1).astype(BF16)
            return 0

        lax.fori_loop(0, n_tiles, part, 0)
        away = pl.ds(pl.multiple_of((1 - core) * r, ROWS), r)
        cores[q] = send(back + q, t.at[cq, away], rcore.at[q], dev_c)

    left = pl.ds(0, h1)
    right = pl.ds(h1, wide - h1)
    hops = back + 4
    hop1, hop2, home = {}, {}, {}
    mine_rows = pl.ds(pl.multiple_of(core * r, ROWS), r)

    def add_core(q):
        cores[q].wait_recv()
        t[chips[q], mine_rows, :] = (
            t[chips[q], mine_rows, :].astype(F32) + rcore[q].astype(F32)
        ).astype(BF16)

    for step in range(experts):
        spread(step)
        if step >= 1:
            relay(step - 1)
        if step >= 2:
            relay_diag(step - 2)
    for c in loads:
        c.wait()
    compute(0)
    relay(experts - 1)
    relay_diag(experts - 2)
    compute(1)
    relay_diag(experts - 1)
    compute(2)
    add_core(1)
    near_x = send(hops + 2, t.at[chip_x, mine_rows, left], rxa, dev_x)
    add_core(2)
    near_y = send(hops + 3, t.at[chip_y, mine_rows, right], rya, dev_y)
    compute(3)
    cores[3].wait_recv()
    for k in range(experts - 1, -1, -1):
        at, zk = rows(zs[k], core), slot(zs[k])
        t[chip_d, at, :] = (
            t[chip_d, at, :].astype(F32) + rcore[3, zk, :].astype(F32)
        ).astype(BF16)
        b = hops + 8 * k
        hop1[k] = (
            send(b, t.at[chip_d, at, left], rxb.at[zk], dev_x),
            send(b + 1, t.at[chip_d, at, right], ryb.at[zk], dev_y),
        )

    def wgrad(i, _):
        at = pl.ds(pl.multiple_of(i * tile, tile), tile)
        res = dot(gut[...], x[:, :, at].reshape(8 * r, tile), 1, 0).astype(BF16).T
        out_gate[at, :] = res[:, :hidden]
        out_up[at, :] = res[:, hidden:]
        return 0

    lax.fori_loop(0, n_tiles, wgrad, 0)
    for k in range(experts - 1, -1, -1):
        at, zk = rows(zs[k], core), slot(zs[k])
        b = hops + 8 * k
        hop1[k][0].wait_recv()
        t[chip_y, at, left] = (t[chip_y, at, left].astype(F32) + rxb[zk, :].astype(F32)).astype(BF16)
        s1 = send(b + 4, t.at[chip_y, at, left], rf1.at[zk], dev_y)
        hop1[k][1].wait_recv()
        t[chip_x, at, right] = (t[chip_x, at, right].astype(F32) + ryb[zk, :].astype(F32)).astype(BF16)
        s2 = send(b + 5, t.at[chip_x, at, right], rf2.at[zk], dev_x)
        hop2[k] = (s1, s2)

    tails = x[:, :, feats:].reshape(8 * r, LANES).astype(F32)
    row_prob = tails[:, 0:1] + tails[:, LANES // 2 : LANES // 2 + 1]

    def dgrad(i, _):
        at = pl.ds(pl.multiple_of(i * tile, tile), tile)
        scaled = (row_prob * g[:, :, at].reshape(8 * r, tile).astype(F32)).astype(BF16)
        out_down[at, :] = dot(hid[...], scaled, 1, 0).astype(BF16).T
        return 0

    lax.fori_loop(0, n_tiles, dgrad, 0)
    cores[0].wait_recv()
    near_x.wait_recv()
    near_y.wait_recv()
    for k in range(experts - 1, -1, -1):
        at, zk = rows(zs[k], core), slot(zs[k])
        for c in hop2[k]:
            c.wait_recv()
        mine = t[chip, at, :].astype(F32) + rcore[0, zk, :].astype(F32)
        lo = mine[:, :h1] + rxa[zk, :].astype(F32) + rf1[zk, :].astype(F32)
        hi = mine[:, h1:] + rya[zk, :].astype(F32) + rf2[zk, :].astype(F32)
        if k > 0:
            t[chip, at, left] = lo.astype(BF16)
            t[chip, at, right] = hi.astype(BF16)
            home[k] = send(hops + 8 * k + 6, t.at[chip, at], o.at[slot(z)], dev_z[k])
        else:
            o[zk, left] = lo.astype(BF16)
            o[zk, right] = hi.astype(BF16)
    for k in range(1, experts):
        home[k].wait_recv()
    out_tokens[...] = dot(place16, o[:, :feats], 0, 0).astype(BF16)
    score = o[:, feats : feats + 1].astype(F32)
    out_probs[0:1, :] = jnp.sum(jnp.where(on0, place, 0.0) * score, axis=0, keepdims=True)
    out_probs[1:2, :] = jnp.sum(jnp.where(on1, place, 0.0) * score, axis=0, keepdims=True)
    for c in started:
        c.wait_send()


def write_out(*refs):
    count = len(refs) // 2
    sems = refs[-1]
    copies = [
        pltpu.make_async_copy(refs[i], refs[count + i], sems.at[i]) for i in range(count)
    ]
    for c in copies:
        c.start()
    for c in copies:
        c.wait()


def finish(arrays):
    arrays = [pltpu.with_memory_space_constraint(a, pltpu.VMEM) for a in arrays]
    return pl.pallas_call(
        write_out,
        out_shape=[jax.ShapeDtypeStruct(a.shape, a.dtype) for a in arrays],
        in_specs=[pl.BlockSpec(memory_space=pltpu.VMEM)] * len(arrays),
        out_specs=[pl.BlockSpec(memory_space=pl.ANY)] * len(arrays),
        scratch_shapes=[pltpu.SemaphoreType.DMA((len(arrays),))],
        compiler_params=pltpu.CompilerParams(has_side_effects=True, vmem_limit_bytes=2**20),
    )(*arrays)


def expert_call(place, limit, experts, cap, tokens, grads, routes, probs, wg, wu, wd):
    toks, feats = tokens.shape
    hidden = wg.shape[1]
    r = experts * cap
    wide = feats + LANES
    h1 = (wide // LANES + 1) // 2 * LANES
    h2 = wide - h1
    vmem = pl.BlockSpec(memory_space=pltpu.VMEM)
    hbm = pl.BlockSpec(memory_space=pltpu.HBM)
    n_sem = experts * 16 + 4 + 8 * experts
    grad = place((feats, hidden), BF16)
    return pl.pallas_call(
        functools.partial(kernel, experts, cap),
        out_shape=(
            place((toks, feats), BF16),
            place((TOP, toks), F32),
            grad,
            grad,
            grad,
        ),
        in_specs=[hbm] * 7,
        out_specs=(vmem,) * 5,
        scratch_shapes=[
            pltpu.VMEM((r, wide), BF16),
            pltpu.VMEM((r, feats), BF16),
            pltpu.VMEM((4, 2 * r, wide), BF16),
            pltpu.VMEM((4, 2 * r, feats), BF16),
            pltpu.VMEM((4, 2 * r, wide), BF16),
            pltpu.VMEM((4, r, wide), BF16),
            pltpu.VMEM((r, h1), BF16),
            pltpu.VMEM((r, h1), BF16),
            pltpu.VMEM((r, h2), BF16),
            pltpu.VMEM((r, h2), BF16),
            pltpu.VMEM((r, h1), BF16),
            pltpu.VMEM((r, h2), BF16),
            pltpu.VMEM((r, wide), BF16),
            pltpu.VMEM((feats, 2 * hidden), BF16),
            pltpu.VMEM((feats, hidden), BF16),
            pltpu.VMEM((2 * hidden, 8 * r), BF16),
            pltpu.VMEM((hidden, 8 * r), BF16),
            pltpu.VMEM((toks, feats), BF16),
            pltpu.VMEM((toks, feats), BF16),
            pltpu.VMEM((TOP, toks), jnp.int32),
            pltpu.VMEM((TOP, toks), F32),
            pltpu.SemaphoreType.DMA((7,)),
            pltpu.SemaphoreType.DMA((n_sem,)),
            pltpu.SemaphoreType.DMA((n_sem,)),
        ],
        compiler_params=pltpu.CompilerParams(
            collective_id=0, has_side_effects=True, vmem_limit_bytes=limit
        ),
    )(tokens, grads, routes, probs, wg, wu, wd)


def per_device(tokens, grad_out, routes, route_probs, gate_weight, up_weight, down_weight):
    tok_count = tokens.shape[0]
    experts = lax.axis_size("ep") // GROUP
    slots = min(
        tok_count // GROUP,
        max(1, (4 * TOP * tok_count + 3 * experts * GROUP - 1) // (3 * experts * GROUP)),
    )
    cap = -(-GROUP * slots // ROWS) * ROWS
    split = lax.axis_size("dp") > 1

    def whole(w):
        return lax.all_gather(w, "dp", axis=1, tiled=True)[0] if split else w[0]

    def shared(term):
        if split:
            term = lax.psum_scatter(term, "dp", scatter_dimension=0, tiled=True)
        return term.astype(BF16)[None]

    made = expert_call(
        jax.ShapeDtypeStruct if split else pltpu.VMEM,
        58 * 2**20 if split else 64100000,
        experts,
        cap,
        tokens,
        grad_out,
        routes.T,
        route_probs.T,
        whole(gate_weight),
        whole(up_weight),
        whole(down_weight),
    )
    grad_tokens, probs, gate, up, down = made if split else finish(made)
    return (grad_tokens, probs.T, shared(gate), shared(up), shared(down))


def solution(mesh):
    rows = P(("ep", "dp"), None)
    blocks = P("ep", "dp", None)
    return jax.shard_map(
        per_device,
        mesh=mesh,
        in_specs=(rows,) * 4 + (blocks,) * 3,
        out_specs=(rows,) * 2 + (blocks,) * 3,
        check_vma=False,
    )
```
